32 devices in a mesh: dp: 32 (over z, y, x, core).
Axes of the slice: x: 2, y: 2, z: 4, core: 2. Of those that a mesh axis runs over, the one named last changes fastest.
Arguments:
- inputs: bfloat16 [31520, 384], P('dp'), may hold values from -6 to 6
- weights: bfloat16 [13824, 128], P('dp'), may hold values from -0.8164966 to 0.8164966
- vectors: float32 [36, 128], replicated, may hold values from -2 to 2
- cotangent: bfloat16 [31520, 384], P('dp'), may hold values from -6 to 6
- mom_weights: float32 [13824, 128], P('dp'), may hold values from -213.046474 to 213.046474
- mom_vectors: float32 [36, 128], replicated, may hold values from -355.07746 to 355.07746
Outputs:
- output: bfloat16 [31520, 384], P('dp')
- grad_inputs: float32 [31520, 384], P('dp')
- grad_weights: float32 [13824, 128], P('dp')
- grad_vectors: float32 [36, 128], replicated
- new_mom_weights: float32 [13824, 128], P('dp')
- new_mom_vectors: float32 [36, 128], replicated
- update_weights: float32 [13824, 128], P('dp')
- update_vectors: float32 [36, 128], replicated
The draws below stay inside these ranges and needn't reach their ends.
All inputs are finite; a program needn't handle non-finite values.
Results may differ from the reference program's by a relative error of at most 0.012.
Values may be sent and summed in bfloat16 or wider, within the bound.
A program may use at most 128 MiB of HBM per device.

```python
import math
import jax
import jax.numpy as jnp
from jax import lax

D = 384
HEADS = 6
HD = 64
FF = 1536
SEQ = 197
IMG_DEV = 5
TOKENS = 31520
WROWS = 13824
VROWS = 36


def draw_weights(key, part):
    own_key = jax.random.fold_in(key, 7101)
    noise = jax.random.truncated_normal(own_key, -4.0, 4.0, (WROWS, 128), jnp.float32)
    row_ids = lax.broadcasted_iota(jnp.int32, (WROWS, 128), 0)
    edge_qkv = 3 * D * D // 128
    edge_out = edge_qkv + D * D // 128
    edge_up = edge_out + D * FF // 128
    factor = jnp.where(row_ids < edge_qkv, D ** (-0.5), jnp.where(row_ids < edge_out, 4.0 * D ** (-0.5), jnp.where(row_ids < edge_up, D ** (-0.5), FF ** (-0.5))))
    return (noise * factor).astype(jnp.bfloat16)


def draw_vectors(key, part):
    own_key = jax.random.fold_in(key, 7202)
    noise = jax.random.truncated_normal(own_key, -4.0, 4.0, (VROWS, 128), jnp.float32)
    position = lax.broadcasted_iota(jnp.int32, (VROWS, 128), 0) * 128 + lax.broadcasted_iota(jnp.int32, (VROWS, 128), 1)
    is_gain = (position < D) | (position >= 5 * D) & (position < 6 * D)
    return jnp.where(is_gain, 1.0 + 0.25 * noise, 0.5 * noise).astype(jnp.float32)


def draw_mom_weights(key, part):
    own_key = jax.random.fold_in(key, 7303)
    noise = jax.random.truncated_normal(own_key, -4.0, 4.0, (WROWS, 128), jnp.float32)
    return (noise * (0.3 * jnp.sqrt(jnp.float32(TOKENS)))).astype(jnp.float32)


def draw_mom_vectors(key, part):
    own_key = jax.random.fold_in(key, 7404)
    noise = jax.random.truncated_normal(own_key, -4.0, 4.0, (VROWS, 128), jnp.float32)
    return (noise * (0.5 * jnp.sqrt(jnp.float32(TOKENS)))).astype(jnp.float32)


def block_levels(key, extent, cuts, smallest, top_value):
    gain = 1.0
    for axis_at, shards_of in cuts:
        draws = jax.random.uniform(jax.random.fold_in(jax.random.fold_in(key, 6), axis_at), (shards_of,), jnp.float32, smallest / len(cuts), top_value / len(cuts))
        gain = gain * jnp.repeat(jnp.exp(draws), extent[axis_at] // shards_of).reshape((-1,) + (1,) * (len(extent) - 1 - axis_at))
    return gain


def normal_values(key, shape, scale, bound, cuts=(), held_as=jnp.bfloat16):
    array = scale * jax.random.normal(key, shape, jnp.float32)
    if cuts:
        array = array * block_levels(key, shape, cuts, -0.22, 0.18)
    return jnp.clip(array, -bound, bound).astype(held_as)


def setup_inputs(seed: int = 0) -> dict:
    keys = jax.random.split(jax.random.key(seed), 7)
    return {
        "inputs": normal_values(keys[0], (TOKENS, D), 1.0, 6.0, ((0, 32),)),
        "weights": draw_weights(jax.random.fold_in(keys[6], 71), 0),
        "vectors": draw_vectors(jax.random.fold_in(keys[6], 71), 0),
        "cotangent": normal_values(keys[3], (TOKENS, D), 1.0, 6.0, ((0, 32),)),
        "mom_weights": draw_mom_weights(jax.random.fold_in(keys[6], 71), 0),
        "mom_vectors": draw_mom_vectors(jax.random.fold_in(keys[6], 71), 0),
    }


HIGH = lax.Precision.HIGHEST
MOMENTUM = 0.95
MATRIX_RATE = 0.5
VECTOR_RATE = 0.2
NEWTON_COEFFS = (3.4445, -4.775, 2.0315)
NORM_EPS = 1e-06

@jax.custom_vjp
def low(v):
    return lax.optimization_barrier(v.astype(jnp.bfloat16)).astype(jnp.float32)

@jax.custom_vjp
def low_back(v):
    return v

def low_keep(v):
    return (low(v), None)

def low_pass(kept, grad):
    return (grad,)

def back_keep(v):
    return (v, None)

def back_low(kept, grad):
    return (low(grad),)
low.defvjp(low_keep, low_pass)
low_back.defvjp(back_keep, back_low)

def split_matrices(flat):
    flat_line = flat.reshape(-1)
    layout = ((D, 3 * D), (D, D), (D, FF), (FF, D))
    pieces = []
    offset = 0
    for dims_pair in layout:
        entries = dims_pair[0] * dims_pair[1]
        pieces.append(flat_line[offset:offset + entries].reshape(dims_pair))
        offset = offset + entries
    return pieces

def split_vectors(flat):
    flat_line = flat.reshape(-1)
    pieces = []
    offset = 0
    for length_one in (D, D, D, D, D, D, D, D, FF):
        pieces.append(flat_line[offset:offset + length_one])
        offset = offset + length_one
    return pieces

def layer_norm(value, norm_gain, norm_shift):
    center = lax.optimization_barrier(jnp.mean(value, axis=-1, keepdims=True))
    deviation = value - center
    spread = lax.optimization_barrier(jnp.mean(deviation * deviation, axis=-1, keepdims=True))
    return deviation * lax.rsqrt(spread + NORM_EPS) * norm_gain + norm_shift

def forward(matrices, pieces, block_in):
    w_qkv, w_out, w_up, w_down = matrices
    ln1_gain, ln1_shift, bias_q, bias_v, bias_out, ln2_gain, ln2_shift, bias_down, bias_up = pieces
    images = block_in.shape[0] // SEQ
    normed = low(layer_norm(block_in, ln1_gain, ln1_shift))
    bias_qkv = jnp.concatenate([bias_q, jnp.zeros_like(bias_q), bias_v])
    qkv = low(low_back(jnp.dot(normed, w_qkv, precision=HIGH) + bias_qkv))
    qkv = qkv.reshape(images, SEQ, 3, HEADS, HD)
    queries = qkv[:, :, 0]
    key_rows = qkv[:, :, 1]
    values = qkv[:, :, 2]
    scores = jnp.einsum('bqhd,bkhd->bhqk', queries, key_rows, precision=HIGH) * HD ** (-0.5)
    scores = low_back(scores)
    probs_low = low(jax.nn.softmax(scores, axis=-1))
    attended = jnp.einsum('bhqk,bkhd->bqhd', probs_low, values, precision=HIGH).reshape(images * SEQ, D)
    attended = low(low_back(attended))
    branch = low_back(jnp.dot(attended, w_out, precision=HIGH) + bias_out)
    middle = block_in + branch
    normed_two = low(layer_norm(middle, ln2_gain, ln2_shift))
    hidden = low_back(jnp.dot(normed_two, w_up, precision=HIGH) + bias_up)
    active = low(jax.nn.gelu(hidden, approximate=False))
    branch_two = low_back(jnp.dot(active, w_down, precision=HIGH) + bias_down)
    return middle + branch_two

def orthogonalize(matrix):
    tall = matrix.shape[0] > matrix.shape[1]
    current = matrix.T if tall else matrix
    current = current / (jnp.sqrt(jnp.sum(current * current)) + 1e-07)
    first, second, third = NEWTON_COEFFS
    for repeat in range(5):
        square = jnp.dot(current, current.T, precision=HIGH)
        poly = second * square + third * jnp.dot(square, square, precision=HIGH)
        current = first * current + jnp.dot(poly, current, precision=HIGH)
    return current.T if tall else current

def reference(inputs, weights, vectors, cotangent, mom_weights, mom_vectors):
    matrices = split_matrices(weights.astype(jnp.float32))
    pieces = split_vectors(vectors)
    block_rows = 4 * IMG_DEV * SEQ
    blocks = TOKENS // block_rows
    stacked_in = inputs.astype(jnp.float32).reshape(blocks, block_rows, D)
    stacked_cot = cotangent.astype(jnp.float32).reshape(blocks, block_rows, D)

    def one_block(totals, pair):
        block_in, block_cot = pair
        result, pull = jax.vjp(forward, matrices, pieces, block_in)
        grad_mats, grad_vecs, grad_in = pull(block_cot)
        totals = jax.tree.map(jnp.add, totals, (grad_mats, grad_vecs))
        return (totals, (result.astype(jnp.bfloat16), grad_in))
    zeros_init = jax.tree.map(jnp.zeros_like, (matrices, pieces))
    totals, outs_pair = lax.scan(one_block, zeros_init, (stacked_in, stacked_cot))
    grad_mats, grad_vecs = totals
    outputs, grad_in = outs_pair
    output = outputs.reshape(TOKENS, D)
    grad_inputs = grad_in.reshape(TOKENS, D)
    grad_weights = jnp.concatenate([item.reshape(-1) for item in grad_mats]).reshape(WROWS, 128)
    grad_vectors = jnp.concatenate(grad_vecs).reshape(VROWS, 128)
    new_mom_weights = MOMENTUM * mom_weights + grad_weights
    new_mom_vectors = MOMENTUM * mom_vectors + grad_vectors
    ortho_list = [orthogonalize(item) for item in split_matrices(new_mom_weights)]
    orthogonal = jnp.concatenate([item.reshape(-1) for item in ortho_list]).reshape(WROWS, 128)
    update_weights = -MATRIX_RATE * orthogonal
    update_vectors = -(VECTOR_RATE / math.sqrt(TOKENS)) * new_mom_vectors
    return (output, grad_inputs, grad_weights, grad_vectors, new_mom_weights, new_mom_vectors, update_weights, update_vectors)
```

```python
import functools
import math

import jax
import jax.numpy as jnp
from jax import lax
from jax.experimental import pallas as pl
from jax.experimental.pallas import tpu as pltpu
from jax.sharding import PartitionSpec as P

D = 384
HEADS = 6
HD = 64
FF = 1536
SEQ = 197


HIGH = lax.Precision.HIGHEST
MOMENTUM = 0.95
MATRIX_RATE = 0.5
VECTOR_RATE = 0.2
NEWTON_COEFFS = (3.4445, -4.775, 2.0315)
NORM_EPS = 1e-06


def split_matrices(flat):
    flat_line = flat.reshape(-1)
    layout = ((D, 3 * D), (D, D), (D, FF), (FF, D))
    pieces = []
    offset = 0
    for dims_pair in layout:
        entries = dims_pair[0] * dims_pair[1]
        pieces.append(flat_line[offset : offset + entries].reshape(dims_pair))
        offset = offset + entries
    return pieces


def split_vectors(flat):
    flat_line = flat.reshape(-1)
    pieces = []
    offset = 0
    for length_one in (D, D, D, D, D, D, D, D, FF):
        pieces.append(flat_line[offset : offset + length_one])
        offset = offset + length_one
    return pieces


def layer_norm(value, norm_gain, norm_shift):
    center = jnp.mean(value, axis=-1, keepdims=True)
    deviation = value - center
    spread = jnp.mean(deviation * deviation, axis=-1, keepdims=True)
    return deviation * lax.rsqrt(spread + NORM_EPS) * norm_gain + norm_shift


def gelu_exact(value):
    return jax.nn.gelu(value, approximate=False)


def matmul(left, right):
    return jnp.dot(left, right, preferred_element_type=jnp.float32)


def outer_sum(left, right):
    return lax.dot_general(
        left, right, (((0,), (0,)), ((), ())), preferred_element_type=jnp.float32
    )


def times_transpose(left, right):
    return lax.dot_general(
        left, right, (((1,), (1,)), ((), ())), preferred_element_type=jnp.float32
    )


def column_sums(value):
    return jnp.sum(value.astype(jnp.float32), axis=0)


EDGES = (0, 3 * D * D // 128, 4 * D * D // 128, (4 * D * D + D * FF) // 128, (4 * D * D + 2 * D * FF) // 128)
WIDTHS = (3 * D // 128, D // 128, FF // 128, D // 128)


def split_low(value):
    high = value.astype(jnp.bfloat16)
    return high, (value - high.astype(jnp.float32)).astype(jnp.bfloat16)


def dot_split(left, right, dims=((1,), (0,))):
    def one(a, b):
        return lax.dot_general(a, b, (dims, ((), ())), preferred_element_type=jnp.float32)

    return one(left[0], right[0]) + (one(left[0], right[1]) + one(left[1], right[0]))


def polar_kernel(rows, mom_ref, out_ref, flat, x_high, x_low, gram, poly_total):
    first_row = lax.axis_index("dp") * rows
    first, second, third = NEWTON_COEFFS
    eye = (
        lax.broadcasted_iota(jnp.int32, (D, D), 0) == lax.broadcasted_iota(jnp.int32, (D, D), 1)
    ).astype(jnp.float32)

    def run(slot):
        low_edge, high_edge, width = EDGES[slot], EDGES[slot + 1], WIDTHS[slot]
        height = (high_edge - low_edge) // width
        tall = height > D
        wide = height if tall else width * 128
        total = jnp.zeros((1, 128), jnp.float32)
        for block in range(width):
            piece = mom_ref[pl.ds(low_edge + block, height, stride=width), :]
            total = total + jnp.sum(piece * piece, axis=0, keepdims=True)
            if tall:
                piece = piece.T
                at = (slice(block * 128, block * 128 + 128), slice(0, height))
            else:
                at = (slice(0, height), slice(block * 128, block * 128 + 128))
            high, low = split_low(piece)
            x_high[at] = high
            x_low[at] = low
        norm = jnp.sqrt(jnp.sum(total)) + 1e-07
        inverse = 1.0 / norm
        whole = (x_high[:, :wide], x_low[:, :wide])
        gram[...] = dot_split(whole, whole, ((1,), (1,))) * (inverse * inverse)
        poly_total[...] = eye

        def step(_, carry):
            square = gram[...]
            square_parts = split_low(square)
            poly = first * eye + second * square + third * dot_split(square_parts, square_parts)
            poly_parts = split_low(poly)
            poly_total[...] = dot_split(poly_parts, split_low(poly_total[...]))
            half = dot_split(poly_parts, square_parts)
            gram[...] = dot_split(split_low(half), poly_parts)
            return carry

        lax.fori_loop(0, 5, step, 0)
        total_parts = split_low(poly_total[...] * (inverse * -MATRIX_RATE))
        for block in range(width):
            if tall:
                lines = slice(block * 128, block * 128 + 128)
                some = (total_parts[0][lines], total_parts[1][lines])
                done = dot_split(some, (x_high[:, :wide], x_low[:, :wide])).T
            else:
                lines = slice(block * 128, block * 128 + 128)
                done = dot_split(total_parts, (x_high[:, lines], x_low[:, lines]))
            flat[pl.ds(low_edge + block, height, stride=width), :] = done

    for slot in range(4):
        needed = jnp.logical_and(
            first_row < EDGES[slot + 1], first_row + rows > EDGES[slot]
        )
        pl.when(needed)(lambda slot=slot: run(slot))
    out_ref[...] = flat[pl.ds(first_row, rows), :]


def polar_update(mom, rows):
    return pl.pallas_call(
        functools.partial(polar_kernel, rows),
        out_shape=jax.ShapeDtypeStruct((rows, 128), jnp.float32),
        in_specs=[pl.BlockSpec(memory_space=pltpu.VMEM)],
        out_specs=pl.BlockSpec(memory_space=pltpu.VMEM),
        scratch_shapes=[
            pltpu.VMEM(mom.shape, jnp.float32),
            pltpu.VMEM((D, FF), jnp.bfloat16),
            pltpu.VMEM((D, FF), jnp.bfloat16),
            pltpu.VMEM((D, D), jnp.float32),
            pltpu.VMEM((D, D), jnp.float32),
        ],
        compiler_params=pltpu.CompilerParams(vmem_limit_bytes=48 * 1024 * 1024),
        name="polar",
    )(mom)


def on_device(inputs, weights, vectors, cotangent, mom_weights, mom_vectors):
    count = lax.axis_size("dp")
    whole = lax.all_gather(weights, "dp", axis=0, tiled=True)
    w_qkv, w_out, w_up, w_down = split_matrices(whole)
    ln1_gain, ln1_shift, bias_q, bias_v, bias_out, ln2_gain, ln2_shift, bias_down, bias_up = (
        split_vectors(vectors)
    )
    rows = inputs.shape[0]
    images = rows // SEQ
    scale_qk = HD ** (-0.5)
    residual_in = inputs.astype(jnp.float32)
    normed, norm_pull = jax.vjp(layer_norm, residual_in, ln1_gain, ln1_shift)
    normed_low = normed.astype(jnp.bfloat16)
    bias_qkv = jnp.concatenate([bias_q, jnp.zeros_like(bias_q), bias_v])
    qkv = (
        (matmul(normed_low, w_qkv) + bias_qkv)
        .astype(jnp.bfloat16)
        .reshape(images, SEQ, 3, HEADS, HD)
    )
    queries = qkv[:, :, 0]
    key_rows = qkv[:, :, 1]
    values = qkv[:, :, 2]
    scores = (
        jnp.einsum("bqhd,bkhd->bhqk", queries, key_rows, preferred_element_type=jnp.float32)
        * scale_qk
    )
    row_max = jnp.max(scores, axis=-1, keepdims=True)
    log_total = row_max + jnp.log(jnp.sum(jnp.exp(scores - row_max), axis=-1, keepdims=True))
    probs_low = jnp.exp(scores - log_total).astype(jnp.bfloat16)
    attended = jnp.einsum("bhqk,bkhd->bqhd", probs_low, values, preferred_element_type=jnp.float32)
    attended = attended.reshape(rows, D).astype(jnp.bfloat16)
    middle = residual_in + matmul(attended, w_out) + bias_out
    normed_two, norm_pull_two = jax.vjp(layer_norm, middle, ln2_gain, ln2_shift)
    normed_two_low = normed_two.astype(jnp.bfloat16)
    hidden = matmul(normed_two_low, w_up) + bias_up
    unused_out, gelu_pull = jax.vjp(gelu_exact, hidden)
    active = gelu_exact(hidden).astype(jnp.bfloat16)
    result = middle + matmul(active, w_down) + bias_down
    output = result.astype(jnp.bfloat16)
    again = lax.all_gather(weights, "dp", axis=0, tiled=True)
    w_qkv, w_out, w_up, w_down = split_matrices(again)
    grad_down = outer_sum(active, cotangent)
    grad_bias_down = column_sums(cotangent)
    d_active = times_transpose(cotangent, w_down)
    d_hidden = gelu_pull(d_active)[0].astype(jnp.bfloat16)
    grad_up = outer_sum(normed_two_low, d_hidden)
    grad_bias_up = column_sums(d_hidden)
    d_normed_two = times_transpose(d_hidden, w_up)
    d_middle_norm, grad_ln2_gain, grad_ln2_shift = norm_pull_two(d_normed_two)
    d_middle = cotangent.astype(jnp.float32) + d_middle_norm
    d_branch = d_middle.astype(jnp.bfloat16)
    grad_out = outer_sum(attended, d_branch)
    grad_bias_out = column_sums(d_branch)
    d_attended = (
        times_transpose(d_branch, w_out).astype(jnp.bfloat16).reshape(images, SEQ, HEADS, HD)
    )
    scores_again = (
        jnp.einsum("bqhd,bkhd->bhqk", queries, key_rows, preferred_element_type=jnp.float32)
        * scale_qk
    )
    probs_full = jnp.exp(scores_again - log_total)
    probs_again = probs_full.astype(jnp.bfloat16)
    grad_values = jnp.einsum(
        "bhqk,bqhd->bkhd", probs_again, d_attended, preferred_element_type=jnp.float32
    )
    d_probs = jnp.einsum("bqhd,bkhd->bhqk", d_attended, values, preferred_element_type=jnp.float32)
    d_scores = probs_full * (d_probs - jnp.sum(d_probs * probs_full, axis=-1, keepdims=True))
    d_scores = d_scores.astype(jnp.bfloat16)
    grad_queries = (
        jnp.einsum("bhqk,bkhd->bqhd", d_scores, key_rows, preferred_element_type=jnp.float32)
        * scale_qk
    )
    grad_keys = (
        jnp.einsum("bhqk,bqhd->bkhd", d_scores, queries, preferred_element_type=jnp.float32)
        * scale_qk
    )
    d_qkv = (
        jnp.stack([grad_queries, grad_keys, grad_values], axis=2)
        .astype(jnp.bfloat16)
        .reshape(rows, 3 * D)
    )
    grad_qkv = outer_sum(normed_low, d_qkv)
    grad_bias_q = column_sums(d_qkv[:, :D])
    grad_bias_v = column_sums(d_qkv[:, 2 * D :])
    d_normed = times_transpose(d_qkv, w_qkv)
    d_input_norm, grad_ln1_gain, grad_ln1_shift = norm_pull(d_normed)
    grad_inputs = d_middle + d_input_norm
    local_grads = jnp.concatenate(
        [grad_qkv.reshape(-1), grad_out.reshape(-1), grad_up.reshape(-1), grad_down.reshape(-1)]
    )
    local_grads = local_grads.reshape(-1, 128)
    local_vector_grads = jnp.concatenate(
        [
            grad_ln1_gain,
            grad_ln1_shift,
            grad_bias_q,
            grad_bias_v,
            grad_bias_out,
            grad_ln2_gain,
            grad_ln2_shift,
            grad_bias_down,
            grad_bias_up,
        ]
    ).reshape(-1, 128)
    grad_vectors = jnp.sum(lax.all_gather(local_vector_grads, "dp"), axis=0)
    grad_weights = lax.psum_scatter(local_grads, "dp", scatter_dimension=0, tiled=True)
    new_mom_weights = MOMENTUM * mom_weights + grad_weights
    gathered = lax.all_gather(new_mom_weights, "dp", axis=0, tiled=True)
    new_mom_vectors = MOMENTUM * mom_vectors + grad_vectors
    update_weights = polar_update(gathered, mom_weights.shape[0])
    total_tokens = rows * count
    update_vectors = -(VECTOR_RATE / math.sqrt(total_tokens)) * new_mom_vectors
    return (
        output,
        grad_inputs,
        grad_weights,
        grad_vectors,
        new_mom_weights,
        new_mom_vectors,
        update_weights,
        update_vectors,
    )


def solution(mesh):
    in_specs = (P("dp", None), P("dp", None), P(), P("dp", None), P("dp", None), P())
    out_specs = (
        P("dp", None),
        P("dp", None),
        P("dp", None),
        P(),
        P("dp", None),
        P(),
        P("dp", None),
        P(),
    )
    return jax.shard_map(
        on_device, mesh=mesh, in_specs=in_specs, out_specs=out_specs, check_vma=False
    )
```

```python
import functools
import math

import jax
import jax.numpy as jnp
from jax import lax
from jax.experimental import pallas as pl
from jax.experimental.pallas import tpu as pltpu
from jax.sharding import PartitionSpec as P

D = 384
HEADS = 6
HD = 64
FF = 1536
SEQ = 197


HIGH = lax.Precision.HIGHEST
MOMENTUM = 0.95
MATRIX_RATE = 0.5
VECTOR_RATE = 0.2
NEWTON_COEFFS = (3.4445, -4.775, 2.0315)
NORM_EPS = 1e-06


def split_matrices(flat):
    flat_line = flat.reshape(-1)
    layout = ((D, 3 * D), (D, D), (D, FF), (FF, D))
    pieces = []
    offset = 0
    for dims_pair in layout:
        entries = dims_pair[0] * dims_pair[1]
        pieces.append(flat_line[offset : offset + entries].reshape(dims_pair))
        offset = offset + entries
    return pieces


def split_vectors(flat):
    flat_line = flat.reshape(-1)
    pieces = []
    offset = 0
    for length_one in (D, D, D, D, D, D, D, D, FF):
        pieces.append(flat_line[offset : offset + length_one])
        offset = offset + length_one
    return pieces


def layer_norm(value, norm_gain, norm_shift):
    center = jnp.mean(value, axis=-1, keepdims=True)
    deviation = value - center
    spread = jnp.mean(deviation * deviation, axis=-1, keepdims=True)
    return deviation * lax.rsqrt(spread + NORM_EPS) * norm_gain + norm_shift


def gelu_exact(value):
    return jax.nn.gelu(value, approximate=False)


def matmul(left, right):
    return jnp.dot(left, right, preferred_element_type=jnp.float32)


def outer_sum(left, right):
    return lax.dot_general(
        left, right, (((0,), (0,)), ((), ())), preferred_element_type=jnp.float32
    )


def times_transpose(left, right):
    return lax.dot_general(
        left, right, (((1,), (1,)), ((), ())), preferred_element_type=jnp.float32
    )


def column_sums(value):
    return jnp.sum(value.astype(jnp.float32), axis=0)


EDGES = (0, 3 * D * D // 128, 4 * D * D // 128, (4 * D * D + D * FF) // 128, (4 * D * D + 2 * D * FF) // 128)
WIDTHS = (3 * D // 128, D // 128, FF // 128, D // 128)


def split_low(value):
    high = value.astype(jnp.bfloat16)
    return high, (value - high.astype(jnp.float32)).astype(jnp.bfloat16)


def dot_split(left, right, dims=((1,), (0,))):
    def one(a, b):
        return lax.dot_general(a, b, (dims, ((), ())), preferred_element_type=jnp.float32)

    return one(left[0], right[0]) + (one(left[0], right[1]) + one(left[1], right[0]))


def polar_kernel(rows, mom_ref, out_ref, flat, x_high, x_low, gram, poly_total):
    first_row = lax.axis_index("dp") * rows
    first, second, third = NEWTON_COEFFS
    eye = (
        lax.broadcasted_iota(jnp.int32, (D, D), 0) == lax.broadcasted_iota(jnp.int32, (D, D), 1)
    ).astype(jnp.float32)

    def run(slot):
        low_edge, high_edge, width = EDGES[slot], EDGES[slot + 1], WIDTHS[slot]
        height = (high_edge - low_edge) // width
        tall = height > D
        wide = height if tall else width * 128
        total = jnp.zeros((1, 128), jnp.float32)
        for block in range(width):
            piece = mom_ref[pl.ds(low_edge + block, height, stride=width), :]
            total = total + jnp.sum(piece * piece, axis=0, keepdims=True)
            if tall:
                piece = piece.T
                at = (slice(block * 128, block * 128 + 128), slice(0, height))
            else:
                at = (slice(0, height), slice(block * 128, block * 128 + 128))
            high, low = split_low(piece)
            x_high[at] = high
            x_low[at] = low
        norm = jnp.sqrt(jnp.sum(total)) + 1e-07
        inverse = 1.0 / norm
        whole = (x_high[:, :wide], x_low[:, :wide])
        gram[...] = dot_split(whole, whole, ((1,), (1,))) * (inverse * inverse)
        poly_total[...] = eye

        def step(_, carry):
            square = gram[...]
            square_parts = split_low(square)
            poly = first * eye + second * square + third * dot_split(square_parts, square_parts)
            poly_parts = split_low(poly)
            poly_total[...] = dot_split(poly_parts, split_low(poly_total[...]))
            half = dot_split(poly_parts, square_parts)
            gram[...] = dot_split(split_low(half), poly_parts)
            return carry

        lax.fori_loop(0, 5, step, 0)
        total_parts = split_low(poly_total[...] * (inverse * -MATRIX_RATE))
        for block in range(width):
            if tall:
                lines = slice(block * 128, block * 128 + 128)
                some = (total_parts[0][lines], total_parts[1][lines])
                done = dot_split(some, (x_high[:, :wide], x_low[:, :wide])).T
            else:
                lines = slice(block * 128, block * 128 + 128)
                done = dot_split(total_parts, (x_high[:, lines], x_low[:, lines]))
            flat[pl.ds(low_edge + block, height, stride=width), :] = done

    for slot in range(4):
        needed = jnp.logical_and(
            first_row < EDGES[slot + 1], first_row + rows > EDGES[slot]
        )
        pl.when(needed)(lambda slot=slot: run(slot))
    out_ref[...] = flat[pl.ds(first_row, rows), :]


def polar_update(mom, rows):
    return pl.pallas_call(
        functools.partial(polar_kernel, rows),
        out_shape=jax.ShapeDtypeStruct((rows, 128), jnp.float32),
        in_specs=[pl.BlockSpec(memory_space=pltpu.VMEM)],
        out_specs=pl.BlockSpec(memory_space=pltpu.VMEM),
        scratch_shapes=[
            pltpu.VMEM(mom.shape, jnp.float32),
            pltpu.VMEM((D, FF), jnp.bfloat16),
            pltpu.VMEM((D, FF), jnp.bfloat16),
            pltpu.VMEM((D, D), jnp.float32),
            pltpu.VMEM((D, D), jnp.float32),
        ],
        compiler_params=pltpu.CompilerParams(vmem_limit_bytes=48 * 1024 * 1024),
        name="polar",
    )(mom)


def exchange(value, bit, count):
    return lax.ppermute(value, "dp", [(i, i ^ (1 << bit)) for i in range(count)])


def bit_orders(count):
    top = count.bit_length() - 2
    order_a = list(range(top))
    order_b = [0, 2, 1] + order_a[3:]
    return top, order_a, order_b


def scatter_sum(blocks, count):
    index = lax.axis_index("dp")
    top, order_a, order_b = bit_orders(count)
    shape = blocks.shape[1:]
    whole = blocks.reshape((2,) * (top + 1) + shape)
    parts = [whole[0], whole[1]]
    lives = [list(range(top - 1, -1, -1)) for _ in range(2)]
    for bits in zip(order_a, order_b):
        for which, bit in enumerate(bits):
            axis = lives[which].index(bit)
            mine = (index >> bit) & 1
            keep = lax.dynamic_index_in_dim(parts[which], mine, axis, keepdims=False)
            send = lax.dynamic_index_in_dim(parts[which], 1 - mine, axis, keepdims=False)
            got = exchange(send.astype(jnp.bfloat16), bit, count)
            parts[which] = keep.astype(jnp.float32) + got.astype(jnp.float32)
            lives[which].remove(bit)
    low_half = ((index >> top) & 1) == 0
    keep = jnp.where(low_half, parts[0], parts[1])
    send = jnp.where(low_half, parts[1], parts[0])
    return keep + exchange(send.astype(jnp.bfloat16), top, count).astype(jnp.float32)


def gather_blocks(block, count):
    index = lax.axis_index("dp")
    top, order_a, order_b = bit_orders(count)
    got = exchange(block, top, count)
    low_half = ((index >> top) & 1) == 0
    parts = [jnp.where(low_half, block, got), jnp.where(low_half, got, block)]
    lives = [[], []]
    for bits in zip(order_a[::-1], order_b[::-1]):
        for which, bit in enumerate(bits):
            got = exchange(parts[which], bit, count)
            live = sorted(lives[which] + [bit], reverse=True)
            axis = live.index(bit)
            is_low = ((index >> bit) & 1) == 0
            first = jnp.where(is_low, parts[which], got)
            second = jnp.where(is_low, got, parts[which])
            parts[which] = jnp.stack([first, second], axis=axis)
            lives[which] = live
    return jnp.stack(parts).reshape((count * block.shape[0],) + block.shape[1:])


def on_device(inputs, weights, vectors, cotangent, mom_weights, mom_vectors):
    count = lax.axis_size("dp")
    whole = lax.all_gather(weights, "dp", axis=0, tiled=True)
    w_qkv, w_out, w_up, w_down = split_matrices(whole)
    ln1_gain, ln1_shift, bias_q, bias_v, bias_out, ln2_gain, ln2_shift, bias_down, bias_up = (
        split_vectors(vectors)
    )
    rows = inputs.shape[0]
    images = rows // SEQ
    scale_qk = HD ** (-0.5)
    residual_in = inputs.astype(jnp.float32)
    normed, norm_pull = jax.vjp(layer_norm, residual_in, ln1_gain, ln1_shift)
    normed_low = normed.astype(jnp.bfloat16)
    bias_qkv = jnp.concatenate([bias_q, jnp.zeros_like(bias_q), bias_v])
    qkv = (
        (matmul(normed_low, w_qkv) + bias_qkv)
        .astype(jnp.bfloat16)
        .reshape(images, SEQ, 3, HEADS, HD)
    )
    queries = qkv[:, :, 0]
    key_rows = qkv[:, :, 1]
    values = qkv[:, :, 2]
    scores = (
        jnp.einsum("bqhd,bkhd->bhqk", queries, key_rows, preferred_element_type=jnp.float32)
        * scale_qk
    )
    row_max = jnp.max(scores, axis=-1, keepdims=True)
    log_total = row_max + jnp.log(jnp.sum(jnp.exp(scores - row_max), axis=-1, keepdims=True))
    probs_low = jnp.exp(scores - log_total).astype(jnp.bfloat16)
    attended = jnp.einsum("bhqk,bkhd->bqhd", probs_low, values, preferred_element_type=jnp.float32)
    attended = attended.reshape(rows, D).astype(jnp.bfloat16)
    middle = residual_in + matmul(attended, w_out) + bias_out
    normed_two, norm_pull_two = jax.vjp(layer_norm, middle, ln2_gain, ln2_shift)
    normed_two_low = normed_two.astype(jnp.bfloat16)
    hidden = matmul(normed_two_low, w_up) + bias_up
    unused_out, gelu_pull = jax.vjp(gelu_exact, hidden)
    active = gelu_exact(hidden).astype(jnp.bfloat16)
    result = middle + matmul(active, w_down) + bias_down
    output = result.astype(jnp.bfloat16)
    again = lax.all_gather(weights, "dp", axis=0, tiled=True)
    w_qkv, w_out, w_up, w_down = split_matrices(again)
    grad_down = outer_sum(active, cotangent)
    grad_bias_down = column_sums(cotangent)
    d_active = times_transpose(cotangent, w_down)
    d_hidden = gelu_pull(d_active)[0].astype(jnp.bfloat16)
    grad_up = outer_sum(normed_two_low, d_hidden)
    grad_bias_up = column_sums(d_hidden)
    d_normed_two = times_transpose(d_hidden, w_up)
    d_middle_norm, grad_ln2_gain, grad_ln2_shift = norm_pull_two(d_normed_two)
    d_middle = cotangent.astype(jnp.float32) + d_middle_norm
    d_branch = d_middle.astype(jnp.bfloat16)
    grad_out = outer_sum(attended, d_branch)
    grad_bias_out = column_sums(d_branch)
    d_attended = (
        times_transpose(d_branch, w_out).astype(jnp.bfloat16).reshape(images, SEQ, HEADS, HD)
    )
    scores_again = (
        jnp.einsum("bqhd,bkhd->bhqk", queries, key_rows, preferred_element_type=jnp.float32)
        * scale_qk
    )
    probs_full = jnp.exp(scores_again - log_total)
    probs_again = probs_full.astype(jnp.bfloat16)
    grad_values = jnp.einsum(
        "bhqk,bqhd->bkhd", probs_again, d_attended, preferred_element_type=jnp.float32
    )
    d_probs = jnp.einsum("bqhd,bkhd->bhqk", d_attended, values, preferred_element_type=jnp.float32)
    d_scores = probs_full * (d_probs - jnp.sum(d_probs * probs_full, axis=-1, keepdims=True))
    d_scores = d_scores.astype(jnp.bfloat16)
    grad_queries = (
        jnp.einsum("bhqk,bkhd->bqhd", d_scores, key_rows, preferred_element_type=jnp.float32)
        * scale_qk
    )
    grad_keys = (
        jnp.einsum("bhqk,bqhd->bkhd", d_scores, queries, preferred_element_type=jnp.float32)
        * scale_qk
    )
    d_qkv = (
        jnp.stack([grad_queries, grad_keys, grad_values], axis=2)
        .astype(jnp.bfloat16)
        .reshape(rows, 3 * D)
    )
    grad_qkv = outer_sum(normed_low, d_qkv)
    grad_bias_q = column_sums(d_qkv[:, :D])
    grad_bias_v = column_sums(d_qkv[:, 2 * D :])
    d_normed = times_transpose(d_qkv, w_qkv)
    d_input_norm, grad_ln1_gain, grad_ln1_shift = norm_pull(d_normed)
    grad_inputs = d_middle + d_input_norm
    local_grads = jnp.concatenate(
        [
            item.astype(jnp.bfloat16).reshape(-1)
            for item in (grad_qkv, grad_out, grad_up, grad_down)
        ]
    )
    local_grads = local_grads.reshape(-1, 128)
    local_vector_grads = jnp.concatenate(
        [
            grad_ln1_gain,
            grad_ln1_shift,
            grad_bias_q,
            grad_bias_v,
            grad_bias_out,
            grad_ln2_gain,
            grad_ln2_shift,
            grad_bias_down,
            grad_bias_up,
        ]
    ).reshape(-1, 128)
    grad_vectors = jnp.sum(lax.all_gather(local_vector_grads, "dp"), axis=0)
    if count >= 8 and count & (count - 1) == 0:
        grad_weights = scatter_sum(local_grads.reshape(count, -1, 128), count)
    else:
        grad_weights = lax.psum_scatter(
            local_grads.astype(jnp.float32), "dp", scatter_dimension=0, tiled=True
        )
    new_mom_weights = MOMENTUM * mom_weights + grad_weights
    gathered = lax.all_gather(new_mom_weights, "dp", axis=0, tiled=True)
    new_mom_vectors = MOMENTUM * mom_vectors + grad_vectors
    update_weights = polar_update(gathered, mom_weights.shape[0])
    total_tokens = rows * count
    update_vectors = -(VECTOR_RATE / math.sqrt(total_tokens)) * new_mom_vectors
    return (
        output,
        grad_inputs,
        grad_weights,
        grad_vectors,
        new_mom_weights,
        new_mom_vectors,
        update_weights,
        update_vectors,
    )


def solution(mesh):
    in_specs = (P("dp", None), P("dp", None), P(), P("dp", None), P("dp", None), P())
    out_specs = (
        P("dp", None),
        P("dp", None),
        P("dp", None),
        P(),
        P("dp", None),
        P(),
        P("dp", None),
        P(),
    )
    return jax.shard_map(
        on_device, mesh=mesh, in_specs=in_specs, out_specs=out_specs, check_vma=False
    )
```
